256 devices in a mesh: section: 2 (over core), row: 8 (over z), col: 16 (over y, x).
Axes of the slice: x: 4, y: 4, z: 8, core: 2. Of those that a mesh axis runs over, the one named last changes fastest.
Arguments:
- hidden_in: bfloat16 [2, 1024, 8192], P('section', 'col', 'row'), may hold values from -80 to 80
- norm_gain: float32 [2, 8192], P('section', 'row'), may hold values from 0.1 to 1.9
- gate_saved: bfloat16 [2, 1024, 14336], P('section', 'row', 'col'), may hold values from -6 to 6
- up_saved: bfloat16 [2, 1024, 14336], P('section', 'row', 'col'), may hold values from -6 to 6
- w_gate: bfloat16 [2, 8192, 14336], P('section', 'row', 'col'), may hold values from -0.0625 to 0.0625
- w_up: bfloat16 [2, 8192, 14336], P('section', 'row', 'col'), may hold values from -0.0625 to 0.0625
- w_down: bfloat16 [2, 14336, 8192], P('section', 'col', 'row'), may hold values from -0.046875 to 0.046875
- out_grad: bfloat16 [1024, 8192], P('col', 'row'), may hold values from -6 to 6
Outputs:
- in_grad: bfloat16 [2, 1024, 8192], P('section', 'col', 'row')
- gain_grad: float32 [2, 8192], P('section', 'row')
- grad_gate: bfloat16 [2, 8192, 14336], P('section', 'row', 'col')
- grad_up: bfloat16 [2, 8192, 14336], P('section', 'row', 'col')
- grad_down: bfloat16 [2, 14336, 8192], P('section', 'col', 'row')
The draws below stay inside these ranges and needn't reach their ends.
All inputs are finite; a program needn't handle non-finite values.
Results may differ from the reference program's by a relative error of at most 0.03.
Values may be sent and summed in bfloat16 or wider, within the bound.
No kernel may reach another device: no remote copies, remote signals or barrier semaphores. Data moves between devices by JAX's collectives and lax.ppermute only.
A program may use at most 128 MiB of HBM per device.

```python
import math
import jax
import jax.numpy as jnp
from jax import lax

D = 8192
FF = 14336
TOKENS = 1024


def draw_hidden_in(key, part):
    key = jax.random.fold_in(key, 7)
    base_key, row_key, col_key = jax.random.split(key, 3)
    shape = (2, TOKENS, D)
    position = jnp.arange(D, dtype=jnp.float32) / D
    base = jnp.clip(jax.random.normal(base_key, shape, jnp.float32), -4.0, 4.0)
    scales = jnp.exp(jax.random.uniform(row_key, (2, TOKENS, 1), jnp.float32, math.log(0.32), math.log(3.2)))
    rising = 10.0 ** (position - 0.5)
    rough = jax.random.uniform(col_key, (2, 1, D), jnp.float32, 0.5, 1.5)
    return (base * scales * rising * rough).astype(jnp.bfloat16)


def levels(key, shape, pieces, smallest, high):
    def one(axis_at, parts):
        steps = jax.random.uniform(jax.random.fold_in(jax.random.fold_in(key, 6), axis_at), (parts,), jnp.float32, smallest / len(pieces), high / len(pieces))
        return jnp.repeat(jnp.exp(steps), shape[axis_at] // parts).reshape((-1,) + (1,) * (len(shape) - axis_at - 1))

    loudness = one(*pieces[0])
    for cut in pieces[1:]:
        loudness = loudness * one(*cut)
    return loudness


def normal_values(own_key, dims, deviation, reach, cuts=(), kind=jnp.bfloat16):
    result = jax.random.normal(own_key, dims, jnp.float32) * deviation
    if len(cuts) > 0:
        result = levels(own_key, dims, cuts, -0.22, 0.18) * result
    return jnp.clip(result, min=-reach, max=reach).astype(kind)


def setup_inputs(seed: int = 0) -> dict:
    key_of = jax.random.split(jax.random.key(seed), 9)
    return {
        "hidden_in": draw_hidden_in(jax.random.fold_in(key_of[8], 71), 0),
        "norm_gain": jnp.clip(1.0 + 0.18 * jax.random.normal(key_of[1], (2, D), jnp.float32), 0.1, 1.9),
        "gate_saved": normal_values(key_of[2], (2, TOKENS, FF), 1.0, 6.0, ((0, 2), (1, 8), (2, 16))),
        "up_saved": normal_values(key_of[3], (2, TOKENS, FF), 1.0, 6.0, ((0, 2), (1, 8), (2, 16))),
        "w_gate": normal_values(key_of[4], (2, D, FF), D ** -0.5, 0.0625, ((0, 2), (1, 8), (2, 16))),
        "w_up": normal_values(key_of[5], (2, D, FF), D ** -0.5, 0.0625, ((0, 2), (1, 8), (2, 16))),
        "w_down": normal_values(key_of[6], (2, FF, D), FF ** -0.5, 0.046875, ((0, 2), (1, 16), (2, 8))),
        "out_grad": normal_values(key_of[7], (TOKENS, D), 1.0, 6.0, ((0, 16), (1, 8))),
    }


epsilon = 1e-05

def layer_backward(hidden, gain, gate_pre, up_vals, gate_w, up_w, down_w, cotangent):
    hidden_f = hidden.astype(jnp.float32)
    inv_rms = lax.rsqrt(lax.optimization_barrier(jnp.sum(hidden_f * hidden_f, axis=1)) / D + epsilon)
    normed = (hidden_f * inv_rms[:, None] * gain).astype(jnp.bfloat16)
    gate_f = gate_pre.astype(jnp.float32)
    up_f = up_vals.astype(jnp.float32)
    sig = jax.nn.sigmoid(gate_f)
    act = (gate_f * sig * up_f).astype(jnp.bfloat16)
    hidden_grad = jnp.dot(cotangent, down_w.T, preferred_element_type=jnp.float32)
    gate_grad = (hidden_grad * up_f * sig * (1.0 + gate_f * (1.0 - sig))).astype(jnp.bfloat16)
    up_grad = (hidden_grad * gate_f * sig).astype(jnp.bfloat16)
    normed_grad = jnp.dot(gate_grad, gate_w.T, preferred_element_type=jnp.float32) + jnp.dot(up_grad, up_w.T, preferred_element_type=jnp.float32)
    cross = lax.optimization_barrier(jnp.sum(gain * normed_grad * hidden_f, axis=1))
    in_grad = (cotangent.astype(jnp.float32) + inv_rms[:, None] * gain * normed_grad - hidden_f * (inv_rms ** 3 * cross / D)[:, None]).astype(jnp.bfloat16)
    gain_grad = lax.optimization_barrier(jnp.sum(normed_grad * hidden_f * inv_rms[:, None], axis=0))
    grad_gate = jnp.dot(normed.T, gate_grad, preferred_element_type=jnp.float32).astype(jnp.bfloat16)
    grad_up = jnp.dot(normed.T, up_grad, preferred_element_type=jnp.float32).astype(jnp.bfloat16)
    grad_down = jnp.dot(act.T, cotangent, preferred_element_type=jnp.float32).astype(jnp.bfloat16)
    return (in_grad, gain_grad, grad_gate, grad_up, grad_down)

def reference(hidden_in, norm_gain, gate_saved, up_saved, w_gate, w_up, w_down, out_grad):
    second = layer_backward(hidden_in[1], norm_gain[1], gate_saved[1], up_saved[1], w_gate[1], w_up[1], w_down[1], out_grad)
    first = layer_backward(hidden_in[0], norm_gain[0], gate_saved[0], up_saved[0], w_gate[0], w_up[0], w_down[0], second[0])
    return (jnp.stack([first[0], second[0]]), jnp.stack([first[1], second[1]]), jnp.stack([first[2], second[2]]), jnp.stack([first[3], second[3]]), jnp.stack([first[4], second[4]]))
```

```python
import jax
import jax.numpy as jnp
from jax import lax
from jax.experimental import pallas as pl
from jax.experimental.pallas import tpu as pltpu
from jax.sharding import PartitionSpec as P

D = 8192
EPSILON = 1e-05

bf16 = jnp.bfloat16
f32 = jnp.float32


def dot(left, right, dims):
    return lax.dot_general(left, right, (dims, ((), ())), preferred_element_type=f32)


def swap(block):
    return lax.ppermute(block, "section", [(0, 1), (1, 0)])


def after(block, event):
    return lax.optimization_barrier((block, event))[0]


def exchange(blocks, axis):
    return lax.all_to_all(blocks, axis, 0, 0)


def spread(block, axis):
    copies = jnp.broadcast_to(block[None], (lax.axis_size(axis),) + block.shape)
    return exchange(copies, axis)


def unit_kernel(hidden_grad, saved, gate_w, up_w, gate_out, up_out, partial):
    grad_f = hidden_grad[...].astype(f32)
    gate_f, up_f = saved[0].astype(f32), saved[1].astype(f32)
    sig = jax.nn.sigmoid(gate_f)
    gate_grad = (grad_f * up_f * sig * (1.0 + gate_f * (1.0 - sig))).astype(bf16)
    up_grad = (grad_f * gate_f * sig).astype(bf16)
    gate_out[...] = gate_grad
    up_out[...] = up_grad
    total = dot(gate_grad, gate_w[...], ((1,), (1,))) + dot(up_grad, up_w[...], ((1,), (1,)))
    partial[...] = total.astype(bf16)


def unit_grads(hidden_grad, saved, gate_w, up_w):
    tokens, units = hidden_grad.shape
    features = gate_w.shape[0]
    tile = 128
    by_tokens = pl.BlockSpec((tile, units), lambda i: (i, 0))
    whole = pl.BlockSpec((features, units), lambda i: (0, 0))
    return pl.pallas_call(
        unit_kernel,
        grid=(tokens // tile,),
        in_specs=[by_tokens, pl.BlockSpec((2, tile, units), lambda i: (0, i, 0)), whole, whole],
        out_specs=[by_tokens, by_tokens, pl.BlockSpec((tile, features), lambda i: (i, 0))],
        out_shape=[
            jax.ShapeDtypeStruct((tokens, units), bf16),
            jax.ShapeDtypeStruct((tokens, units), bf16),
            jax.ShapeDtypeStruct((tokens, features), bf16),
        ],
        compiler_params=pltpu.CompilerParams(vmem_limit_bytes=40 * 1024 * 1024),
        cost_estimate=pl.CostEstimate(
            flops=4 * tokens * units * features,
            bytes_accessed=10 * tokens * units + 4 * units * features + 2 * tokens * features,
            transcendentals=tokens * units,
        ),
    )(hidden_grad, saved, gate_w, up_w)


def body(hidden_in, norm_gain, gate_saved, up_saved, w_gate, w_up, w_down, out_grad):
    rows, cols = lax.axis_size("row"), lax.axis_size("col")
    first = lax.axis_index("section") == 0
    features = hidden_in.shape[2]
    units = gate_saved.shape[2]
    half = hidden_in.shape[1] // 2

    def mine_theirs(block):
        low, high = block[:half], block[half:]
        return jnp.where(first, low, high), jnp.where(first, high, low)

    def by_layer(own, other):
        return jnp.where(first, other, own), jnp.where(first, own, other)

    gate_blocks = gate_saved[0].reshape(2, 2, half, units)
    up_blocks = up_saved[0].reshape(2, 2, half, units)
    saved = jnp.stack([gate_blocks, up_blocks])
    saved_low, saved_high = saved[:, :, 0], saved[:, :, 1]
    saved_mine = jnp.where(first, saved_low, saved_high)
    saved_other = swap(jnp.where(first, saved_high, saved_low))

    def gather_saved(block):
        block = block.reshape(2, 1, 2 * half, units)
        return lax.all_gather(block, "row", axis=2, tiled=True)

    saved1, saved0 = by_layer(saved_mine, saved_other)
    down1, down0 = by_layer(w_down[0], swap(after(w_down[0], saved_other)))
    down1, down0 = after((down1, down0), saved1)
    hid_mine, hid_theirs = mine_theirs(hidden_in[0])
    hid_other = swap(hid_theirs)
    gain1, gain0 = by_layer(norm_gain[0], swap(norm_gain[0]))
    hid1, hid0 = by_layer(hid_mine, hid_other)

    def scatter_units(cot, down_w):
        cot_all = spread(cot, "col").reshape(cols * half, features)
        return cot_all, dot(cot_all, down_w, ((1,), (1,))).astype(bf16)

    def gather_units(partial):
        pieces = exchange(partial.reshape(rows, 2 * half, units), "row")
        return jnp.sum(pieces.astype(f32), axis=0).astype(bf16)

    def all_units(grad_local):
        return spread(grad_local, "row").reshape(cols * half, units)

    def normed_grads(partial):
        pieces = exchange(partial.reshape(cols, half, features), "col")
        return jnp.sum(pieces.astype(f32), axis=0)

    def inner(normed_grad, hidden, gain):
        return jnp.sum(gain * normed_grad * hidden.astype(f32), axis=1)

    def over_rows(sums):
        return jnp.sum(spread(sums.reshape(1, -1), "row"), axis=0)[0]

    def finish(cot, normed_grad, hidden, inv_rms, gain, cross):
        return (
            cot.astype(f32)
            + inv_rms[:, None] * gain * normed_grad
            - hidden.astype(f32) * (inv_rms**3 * cross / D)[:, None]
        ).astype(bf16)

    def gain_part(normed_grad, hidden, inv_rms):
        return jnp.sum(normed_grad * hidden.astype(f32) * inv_rms[:, None], axis=0)

    def activation(saved):
        gate_f = saved[0].astype(f32)
        return (gate_f * jax.nn.sigmoid(gate_f) * saved[1].astype(f32)).astype(bf16)

    def both_halves(layer1, layer0, event):
        layer1, layer0, _ = lax.optimization_barrier((layer1, layer0, event))
        own = jnp.where(first, layer0, layer1)
        other = swap(jnp.where(first, layer1, layer0))
        return jnp.concatenate([own, other], axis=0)

    def handed(block, source, target):
        return lax.ppermute(block, "section", [(source, target)])

    def joined_halves(own1, other1, own0, other0):
        return jnp.concatenate([jnp.where(first, own0, own1), jnp.where(first, other0, other1)], axis=0)

    saved1 = gather_saved(saved1)
    cot1 = mine_theirs(out_grad)[0]
    cot_all1, partial = scatter_units(cot1, down1)
    gate_own, up_own = w_gate[0], w_up[0]
    gate_swapped = swap(after(gate_own, cot_all1))
    up_swapped = swap(after(up_own, cot_all1))
    grad_local = gather_units(partial)
    gates1, gates0 = lax.optimization_barrier(by_layer(gate_own, gate_swapped))
    ups1, ups0 = lax.optimization_barrier(by_layer(up_own, up_swapped))
    both = jnp.concatenate([hid_mine, hid_theirs, hid_other], axis=0).astype(f32)
    squares = after(jnp.sum(both * both, axis=1), grad_local)

    grad_local = after(grad_local, saved1)
    gate_grad1, up_grad1, partial = unit_grads(all_units(grad_local), saved1[:, 0], gates1, ups1)
    saved0 = gather_saved(after(saved0, gate_grad1))
    normed_grad1 = normed_grads(partial)
    sums = over_rows(jnp.concatenate([squares, inner(normed_grad1, hid1, gain1)]))
    inv = lax.rsqrt(sums[: 3 * half] / D + EPSILON)
    inv1, inv0 = by_layer(inv[:half], inv[2 * half :])
    result1 = finish(cot1, normed_grad1, hid1, inv1, gain1, sums[3 * half :])

    cot_all0, partial = scatter_units(result1, down0)
    partial = after(partial, saved0)
    normed = jnp.concatenate([hid_mine, hid_theirs], axis=0).astype(f32)
    normed = normed * inv[: 2 * half, None] * norm_gain[0]
    normed = after(normed.astype(bf16).reshape(2, half, features), cot_all0)
    normed = lax.all_gather(normed, "col", axis=1, tiled=True)
    grad_local = gather_units(partial)
    hidden_grad = all_units(grad_local)
    gate_from_other = handed(after(gate_grad1, cot_all0), 0, 1)
    up_from_other = handed(after(up_grad1, cot_all0), 0, 1)
    cot_both = both_halves(cot_all1, cot_all0, cot_all0)
    act_both = both_halves(activation(saved1[:, 0]), activation(saved0[:, 0]), cot_all0)
    grad_down = dot(act_both, cot_both, ((0,), (0,))).astype(bf16)
    hidden_grad = after(hidden_grad, grad_down)
    gate_grad0, up_grad0, partial = unit_grads(hidden_grad, saved0[:, 0], gates0, ups0)
    partial = after(partial, normed)
    gate_grads = joined_halves(gate_grad1, gate_from_other, gate_grad0, handed(gate_grad0, 1, 0))
    up_grads = joined_halves(up_grad1, up_from_other, up_grad0, handed(up_grad0, 1, 0))
    normed_grad0 = normed_grads(partial)
    cross = over_rows(inner(normed_grad0, hid0, gain0))
    result0 = finish(result1, normed_grad0, hid0, inv0, gain0, cross)

    tokens = 2 * half * cols
    normed = normed.reshape(tokens, features)
    grad_gate = dot(normed, gate_grads, ((0,), (0,))).astype(bf16)
    grad_up = dot(normed, up_grads, ((0,), (0,))).astype(bf16)

    gain1_part = gain_part(normed_grad1, hid1, inv1)
    gain0_part = gain_part(normed_grad0, hid0, inv0)
    gain_parts = jnp.stack([jnp.where(first, gain0_part, gain1_part), jnp.where(first, gain1_part, gain0_part)])
    gain_parts = jnp.sum(spread(gain_parts, "col"), axis=0)
    gain_total = gain_parts[0] + swap(gain_parts[1])
    own = jnp.where(first, result0, result1)
    other = swap(jnp.where(first, result1, result0))
    result = jnp.where(first, jnp.concatenate([own, other]), jnp.concatenate([other, own]))
    return (result[None], gain_total[None], grad_gate[None], grad_up[None], grad_down[None])


def solution(mesh):
    placed = (
        P("section", "col", "row"),
        P("section", "row"),
        P("section", "row", "col"),
        P("section", "row", "col"),
        P("section", "row", "col"),
        P("section", "row", "col"),
        P("section", "col", "row"),
        P("col", "row"),
    )
    return jax.shard_map(
        body,
        mesh=mesh,
        in_specs=placed,
        out_specs=(
            P("section", "col", "row"),
            P("section", "row"),
            P("section", "row", "col"),
            P("section", "row", "col"),
            P("section", "col", "row"),
        ),
        check_vma=False,
    )
```

```python
import jax
import jax.numpy as jnp
from jax import lax
from jax.sharding import PartitionSpec as P

D = 8192
EPSILON = 1e-05

bf16 = jnp.bfloat16
f32 = jnp.float32


def dot(left, right, dims):
    return lax.dot_general(left, right, (dims, ((), ())), preferred_element_type=f32)


def swap(block):
    return lax.ppermute(block, "section", [(0, 1), (1, 0)])


def after(block, event):
    return lax.optimization_barrier((block, event))[0]


def exchange(blocks, axis):
    return lax.all_to_all(blocks, axis, 0, 0)


def spread(block, axis):
    copies = jnp.broadcast_to(block[None], (lax.axis_size(axis),) + block.shape)
    return exchange(copies, axis)


def unit_grads(hidden_grad, saved):
    grad_f = hidden_grad.astype(f32)
    gate_f, up_f = saved[0].astype(f32), saved[1].astype(f32)
    sig = jax.nn.sigmoid(gate_f)
    gate_grad = (grad_f * up_f * sig * (1.0 + gate_f * (1.0 - sig))).astype(bf16)
    up_grad = (grad_f * gate_f * sig).astype(bf16)
    return gate_grad, up_grad


def into_features(gate_grad, up_grad, gate_w, up_w):
    partial = dot(gate_grad, gate_w, ((1,), (1,))) + dot(up_grad, up_w, ((1,), (1,)))
    return partial.astype(bf16)


def body(hidden_in, norm_gain, gate_saved, up_saved, w_gate, w_up, w_down, out_grad):
    rows, cols = lax.axis_size("row"), lax.axis_size("col")
    first = lax.axis_index("section") == 0
    features = hidden_in.shape[2]
    units = gate_saved.shape[2]
    half = hidden_in.shape[1] // 2

    def mine_theirs(block):
        low, high = block[:half], block[half:]
        return jnp.where(first, low, high), jnp.where(first, high, low)

    def by_layer(own, other):
        return jnp.where(first, other, own), jnp.where(first, own, other)

    gate_blocks = gate_saved[0].reshape(2, 2, half, units)
    up_blocks = up_saved[0].reshape(2, 2, half, units)
    saved = jnp.stack([gate_blocks, up_blocks])
    saved_low, saved_high = saved[:, :, 0], saved[:, :, 1]
    saved_mine = jnp.where(first, saved_low, saved_high)
    saved_other = swap(jnp.where(first, saved_high, saved_low))

    def gather_saved(block):
        block = block.reshape(2, 1, 2 * half, units)
        return lax.all_gather(block, "row", axis=2, tiled=True)

    saved1, saved0 = by_layer(saved_mine, saved_other)
    down_own = w_down[0]
    down_swapped = swap(after(down_own, saved_other))
    down1 = after(jnp.where(first, down_swapped, down_own), saved1)
    hid_mine, hid_theirs = mine_theirs(hidden_in[0])
    hid_other = swap(hid_theirs)
    my_col = lax.axis_index("col")
    gain1, gain0 = by_layer(norm_gain[0], swap(norm_gain[0]))
    hid1, hid0 = by_layer(hid_mine, hid_other)

    def scatter_units(cot, down_w):
        cot_all = spread(cot, "col").reshape(cols * half, features)
        return cot_all, dot(cot_all, down_w, ((1,), (1,))).astype(bf16)

    def gather_units(partial):
        pieces = exchange(partial.reshape(rows, 2 * half, units), "row")
        return jnp.sum(pieces.astype(f32), axis=0).astype(bf16)

    def all_units(grad_local):
        return spread(grad_local, "row").reshape(cols * half, units)

    def normed_grads(partial):
        pieces = exchange(partial.reshape(cols, half, features), "col")
        return jnp.sum(pieces.astype(f32), axis=0)

    def inner(partial, hidden, gain):
        return jnp.sum(gain * partial.astype(f32) * hidden.astype(f32), axis=1)

    def over_rows(sums):
        sums = sums.reshape(-1, 128)
        for bit in (1, 2, 4):
            sums = sums + lax.ppermute(sums, "row", [(i, i ^ bit) for i in range(rows)])
        return sums.reshape(-1)

    def own_tokens(values):
        return lax.dynamic_slice(values, (my_col * half,), (half,))

    def inverse(squares):
        return lax.rsqrt(squares / D + EPSILON)

    def without_cross(cot, normed_grad, inv_rms, gain):
        return cot.astype(f32) + inv_rms[:, None] * gain * normed_grad

    def cross_term(hidden, inv_rms, cross):
        return hidden.astype(f32) * (inv_rms**3 * cross / D)[:, None]

    def gain_part(normed_grad, hidden, inv_rms):
        return jnp.sum(normed_grad * hidden.astype(f32) * inv_rms[:, None], axis=0)

    def activation(saved):
        gate_f = saved[0].astype(f32)
        return (gate_f * jax.nn.sigmoid(gate_f) * saved[1].astype(f32)).astype(bf16)

    def both_halves(layer1, layer0, event):
        layer1, layer0, _ = lax.optimization_barrier((layer1, layer0, event))
        own = jnp.where(first, layer0, layer1)
        other = swap(jnp.where(first, layer1, layer0))
        return own, other

    def handed(block, source, target):
        return lax.ppermute(block, "section", [(source, target)])

    saved1 = gather_saved(saved1)
    hid_own = jnp.stack([hid_mine, hid_theirs])
    cot1 = mine_theirs(out_grad)[0]
    cot_all1, partial = scatter_units(cot1, down1)
    hid_own = lax.all_gather(after(hid_own, cot_all1), "col", axis=1, tiled=True)
    hid_back = swap(hid_own[1])
    hid_all1 = jnp.where(first, hid_back, hid_own[0])
    gate_own, up_own = w_gate[0], w_up[0]
    gate_swapped = swap(after(gate_own, cot_all1))
    up_swapped = swap(after(up_own, cot_all1))
    grad_local = gather_units(partial)
    gates1 = lax.optimization_barrier(jnp.where(first, gate_swapped, gate_own))
    ups1 = lax.optimization_barrier(jnp.where(first, up_swapped, up_own))
    squares = [jnp.sum(jnp.square(block.astype(f32)), axis=1) for block in (hid_own[0], hid_own[1], hid_back)]

    hidden_grad1 = all_units(after(grad_local, saved1))
    gate_grad1, up_grad1 = unit_grads(hidden_grad1, saved1[:, 0])
    partial = lax.optimization_barrier(into_features(gate_grad1, up_grad1, gates1, ups1))
    saved0 = gather_saved(after(saved0, gate_grad1))
    normed_grad1 = normed_grads(partial)
    sums = over_rows(jnp.concatenate([inner(partial, hid_all1, gain1)] + squares)).reshape(4, -1)
    inv_mine, inv_theirs, inv_back = inverse(sums[1]), inverse(sums[2]), inverse(sums[3])
    inv_all1, inv_all0 = by_layer(inv_mine, inv_back)
    inv1, inv0 = own_tokens(inv_all1), own_tokens(inv_all0)
    almost1 = without_cross(cot1, normed_grad1, inv1, gain1)

    down0 = jnp.where(first, *lax.optimization_barrier((down_own, down_swapped, almost1))[:2])
    high = lax.optimization_barrier(sums[0].astype(bf16))
    low = (sums[0] - high.astype(f32)).astype(bf16)
    extra = jnp.pad(jnp.concatenate([high, low]).reshape(1, -1), ((0, 7), (0, 0)))
    pieces = spread(jnp.concatenate([almost1.astype(bf16), extra]), "col")
    cross = jnp.sum(pieces[:, half].astype(f32), axis=0).reshape(2, -1)
    cross = cross[0] + cross[1]
    cot_all0 = pieces[:, :half].reshape(cols * half, features).astype(f32)
    cot_all0 = (cot_all0 - cross_term(hid_all1, inv_all1, cross)).astype(bf16)
    result1 = (almost1 - cross_term(hid1, inv1, own_tokens(cross))).astype(bf16)
    partial = dot(cot_all0, lax.optimization_barrier(down0), ((1,), (1,))).astype(bf16)
    partial = after(partial, saved0)
    grad_local = gather_units(partial)
    hidden_grad0 = all_units(grad_local)
    grad_late = handed(hidden_grad0, 1, 0)
    saved_own, saved_theirs = both_halves(saved1[:, 0], saved0[:, 0], cot_all0)
    cot_own, cot_theirs = both_halves(cot_all1, cot_all0, cot_all0)
    grad_early = handed(after(hidden_grad1, cot_all0), 0, 1)
    weights = lax.optimization_barrier((gate_own, gate_swapped, up_own, up_swapped, grad_local))
    gates0 = lax.optimization_barrier(jnp.where(first, weights[0], weights[1]))
    ups0 = lax.optimization_barrier(jnp.where(first, weights[2], weights[3]))
    ready = (saved_theirs, cot_theirs, grad_early, gates0, ups0)
    gate_grad0, up_grad0 = unit_grads(after(hidden_grad0, ready), saved0[:, 0])
    partial = into_features(gate_grad0, up_grad0, gates0, ups0)
    normed_grad0 = normed_grads(partial)
    grad_theirs, saved_own, saved_theirs, cot_own, cot_theirs = after(
        (jnp.where(first, grad_late, grad_early), saved_own, saved_theirs, cot_own, cot_theirs), partial
    )
    gate_theirs, up_theirs = unit_grads(grad_theirs, saved_theirs)
    gate_own, up_own = after(
        (jnp.where(first, gate_grad0, gate_grad1), jnp.where(first, up_grad0, up_grad1)), partial
    )
    gate_grads = jnp.concatenate([gate_own, gate_theirs], axis=0)
    up_grads = jnp.concatenate([up_own, up_theirs], axis=0)
    acts = jnp.concatenate([activation(saved_own), activation(saved_theirs)], axis=0)
    grad_down = dot(acts, jnp.concatenate([cot_own, cot_theirs], axis=0), ((0,), (0,))).astype(bf16)
    cross = spread(jnp.sum(gain0 * normed_grad0 * hid0.astype(f32), axis=1).reshape(1, -1), "row")
    almost0 = without_cross(result1, normed_grad0, inv0, gain0)
    result0 = (almost0 - cross_term(hid0, inv0, jnp.sum(cross, axis=0)[0])).astype(bf16)

    inv_own = jnp.concatenate([inv_mine, inv_theirs])
    normed = hid_own.reshape(2 * half * cols, features).astype(f32) * inv_own[:, None] * norm_gain[0]
    normed = after(normed.astype(bf16), cot_all0)
    grad_gate = dot(normed, gate_grads, ((0,), (0,))).astype(bf16)
    grad_up = dot(normed, up_grads, ((0,), (0,))).astype(bf16)

    gain1_part = gain_part(normed_grad1, hid1, inv1)
    gain0_part = gain_part(normed_grad0, hid0, inv0)
    gain_parts = jnp.stack([jnp.where(first, gain0_part, gain1_part), jnp.where(first, gain1_part, gain0_part)])
    gain_parts = jnp.sum(spread(gain_parts, "col"), axis=0)
    gain_total = gain_parts[0] + swap(gain_parts[1])
    own = jnp.where(first, result0, result1)
    other = swap(jnp.where(first, result1, result0))
    result = jnp.where(first, jnp.concatenate([own, other]), jnp.concatenate([other, own]))
    return (result[None], gain_total[None], grad_gate[None], grad_up[None], grad_down[None])


def solution(mesh):
    placed = (
        P("section", "col", "row"),
        P("section", "row"),
        P("section", "row", "col"),
        P("section", "row", "col"),
        P("section", "row", "col"),
        P("section", "row", "col"),
        P("section", "col", "row"),
        P("col", "row"),
    )
    return jax.shard_map(
        body,
        mesh=mesh,
        in_specs=placed,
        out_specs=(
            P("section", "col", "row"),
            P("section", "row"),
            P("section", "row", "col"),
            P("section", "row", "col"),
            P("section", "col", "row"),
        ),
        check_vma=False,
    )
```

```python
import jax
import jax.numpy as jnp
from jax import lax
from jax.sharding import PartitionSpec as P

D = 8192
EPSILON = 1e-05

bf16 = jnp.bfloat16
f32 = jnp.float32


def dot(left, right, dims):
    return lax.dot_general(left, right, (dims, ((), ())), preferred_element_type=f32)


def swap(block):
    return lax.ppermute(block, "section", [(0, 1), (1, 0)])


def after(block, event):
    return lax.optimization_barrier((block, event))[0]


def exchange(blocks, axis):
    return lax.all_to_all(blocks, axis, 0, 0)


def spread(block, axis):
    copies = jnp.broadcast_to(block[None], (lax.axis_size(axis),) + block.shape)
    return exchange(copies, axis)


def unit_grads(hidden_grad, saved):
    grad_f = hidden_grad.astype(f32)
    gate_f, up_f = saved[0].astype(f32), saved[1].astype(f32)
    sig = jax.nn.sigmoid(gate_f)
    gate_grad = (grad_f * up_f * sig * (1.0 + gate_f * (1.0 - sig))).astype(bf16)
    up_grad = (grad_f * gate_f * sig).astype(bf16)
    return gate_grad, up_grad


def into_features(gate_grad, up_grad, gate_w, up_w):
    partial = dot(gate_grad, gate_w, ((1,), (1,))) + dot(up_grad, up_w, ((1,), (1,)))
    return partial.astype(bf16)


def body(hidden_in, norm_gain, gate_saved, up_saved, w_gate, w_up, w_down, out_grad):
    rows, cols = lax.axis_size("row"), lax.axis_size("col")
    first = lax.axis_index("section") == 0
    features = hidden_in.shape[2]
    units = gate_saved.shape[2]
    half = hidden_in.shape[1] // 2

    def mine_theirs(block):
        low, high = block[:half], block[half:]
        return jnp.where(first, low, high), jnp.where(first, high, low)

    def by_layer(own, other):
        return jnp.where(first, other, own), jnp.where(first, own, other)

    gate_blocks = gate_saved[0].reshape(2, 2, half, units)
    up_blocks = up_saved[0].reshape(2, 2, half, units)
    saved = jnp.stack([gate_blocks, up_blocks])
    saved_low, saved_high = saved[:, :, 0], saved[:, :, 1]
    saved_mine = jnp.where(first, saved_low, saved_high)
    saved_other = swap(jnp.where(first, saved_high, saved_low))

    def gather_saved(block):
        block = block.reshape(2, 1, 2 * half, units)
        return lax.all_gather(block, "row", axis=2, tiled=True)

    saved1, saved0 = by_layer(saved_mine, saved_other)
    down_own = w_down[0]
    down_swapped = swap(after(down_own, saved_other))
    down1 = after(jnp.where(first, down_swapped, down_own), saved1)
    hid_mine, hid_theirs = mine_theirs(hidden_in[0])
    hid_other = swap(hid_theirs)
    gain1, gain0 = by_layer(norm_gain[0], swap(norm_gain[0]))
    hid1, hid0 = by_layer(hid_mine, hid_other)

    def scatter_units(cot, down_w):
        cot_all = spread(cot, "col").reshape(cols * half, features)
        return cot_all, dot(cot_all, down_w, ((1,), (1,))).astype(bf16)

    def gather_units(partial):
        pieces = exchange(partial.reshape(rows, 2 * half, units), "row")
        return jnp.sum(pieces.astype(f32), axis=0).astype(bf16)

    def all_units(grad_local):
        return spread(grad_local, "row").reshape(cols * half, units)

    def normed_grads(partial):
        pieces = exchange(partial.reshape(cols, half, features), "col")
        return jnp.sum(pieces.astype(f32), axis=0)

    def inner(normed_grad, hidden, gain):
        return jnp.sum(gain * normed_grad * hidden.astype(f32), axis=1)

    def over_rows(sums):
        return jnp.sum(spread(sums.reshape(1, -1), "row"), axis=0)[0]

    def finish(cot, normed_grad, hidden, inv_rms, gain, cross):
        return (
            cot.astype(f32)
            + inv_rms[:, None] * gain * normed_grad
            - hidden.astype(f32) * (inv_rms**3 * cross / D)[:, None]
        ).astype(bf16)

    def gain_part(normed_grad, hidden, inv_rms):
        return jnp.sum(normed_grad * hidden.astype(f32) * inv_rms[:, None], axis=0)

    def activation(saved):
        gate_f = saved[0].astype(f32)
        return (gate_f * jax.nn.sigmoid(gate_f) * saved[1].astype(f32)).astype(bf16)

    def both_halves(layer1, layer0, event):
        layer1, layer0, _ = lax.optimization_barrier((layer1, layer0, event))
        own = jnp.where(first, layer0, layer1)
        other = swap(jnp.where(first, layer1, layer0))
        return own, other

    def handed(block, source, target):
        return lax.ppermute(block, "section", [(source, target)])

    saved1 = gather_saved(saved1)
    cot1 = mine_theirs(out_grad)[0]
    cot_all1, partial = scatter_units(cot1, down1)
    gate_own, up_own = w_gate[0], w_up[0]
    gate_swapped = swap(after(gate_own, cot_all1))
    up_swapped = swap(after(up_own, cot_all1))
    grad_local = gather_units(partial)
    gates1 = lax.optimization_barrier(jnp.where(first, gate_swapped, gate_own))
    ups1 = lax.optimization_barrier(jnp.where(first, up_swapped, up_own))
    both = jnp.concatenate([hid_mine, hid_theirs, hid_other], axis=0).astype(f32)
    squares = after(jnp.sum(both * both, axis=1), grad_local)

    grad_local = after(grad_local, saved1)
    hidden_grad1 = all_units(grad_local)
    gate_grad1, up_grad1 = unit_grads(hidden_grad1, saved1[:, 0])
    partial = into_features(gate_grad1, up_grad1, gates1, ups1)
    saved0 = gather_saved(after(saved0, gate_grad1))
    normed_grad1 = normed_grads(partial)
    sums = over_rows(jnp.concatenate([squares, inner(normed_grad1, hid1, gain1)]))
    inv = lax.rsqrt(sums[: 3 * half] / D + EPSILON)
    inv1, inv0 = by_layer(inv[:half], inv[2 * half :])
    result1 = finish(cot1, normed_grad1, hid1, inv1, gain1, sums[3 * half :])

    down0 = jnp.where(first, *lax.optimization_barrier((down_own, down_swapped, result1))[:2])
    cot_all0, partial = scatter_units(result1, lax.optimization_barrier(down0))
    partial = after(partial, saved0)
    normed = jnp.concatenate([hid_mine, hid_theirs], axis=0).astype(f32)
    normed = normed * inv[: 2 * half, None] * norm_gain[0]
    normed = after(normed.astype(bf16).reshape(2, half, features), cot_all0)
    normed = lax.all_gather(normed, "col", axis=1, tiled=True)
    grad_local = gather_units(partial)
    hidden_grad0 = all_units(grad_local)
    grad_late = handed(hidden_grad0, 1, 0)
    saved_own, saved_theirs = both_halves(saved1[:, 0], saved0[:, 0], cot_all0)
    cot_own, cot_theirs = both_halves(cot_all1, cot_all0, cot_all0)
    grad_early = handed(after(hidden_grad1, cot_all0), 0, 1)
    weights = lax.optimization_barrier((gate_own, gate_swapped, up_own, up_swapped, grad_local))
    gates0 = lax.optimization_barrier(jnp.where(first, weights[0], weights[1]))
    ups0 = lax.optimization_barrier(jnp.where(first, weights[2], weights[3]))
    ready = (saved_theirs, cot_theirs, grad_early, gates0, ups0)
    gate_grad0, up_grad0 = unit_grads(after(hidden_grad0, ready), saved0[:, 0])
    partial = after(into_features(gate_grad0, up_grad0, gates0, ups0), normed)
    normed_grad0 = normed_grads(partial)
    grad_theirs = after(jnp.where(first, grad_late, grad_early), partial)
    gate_theirs, up_theirs = unit_grads(grad_theirs, saved_theirs)
    gate_own, up_own = after(
        (jnp.where(first, gate_grad0, gate_grad1), jnp.where(first, up_grad0, up_grad1)), partial
    )
    gate_grads = jnp.concatenate([gate_own, gate_theirs], axis=0)
    up_grads = jnp.concatenate([up_own, up_theirs], axis=0)
    saved_own, saved_late, cot_own, cot_theirs = after((saved_own, saved_theirs, cot_own, cot_theirs), normed_grad0)
    acts = jnp.concatenate([activation(saved_own), activation(saved_late)], axis=0)
    grad_down = dot(acts, jnp.concatenate([cot_own, cot_theirs], axis=0), ((0,), (0,))).astype(bf16)
    cross = inner(normed_grad0, hid0, gain0)
    for bit in (1, 2, 4):
        cross = cross + lax.ppermute(cross, "row", [(i, i ^ bit) for i in range(rows)])
    result0 = finish(result1, normed_grad0, hid0, inv0, gain0, cross)

    tokens = 2 * half * cols
    normed = normed.reshape(tokens, features)
    grad_gate = dot(normed, gate_grads, ((0,), (0,))).astype(bf16)
    grad_up = dot(normed, up_grads, ((0,), (0,))).astype(bf16)

    gain1_part = gain_part(normed_grad1, hid1, inv1)
    gain0_part = gain_part(normed_grad0, hid0, inv0)
    gain_parts = jnp.stack([jnp.where(first, gain0_part, gain1_part), jnp.where(first, gain1_part, gain0_part)])
    gain_parts = jnp.sum(after(spread(gain_parts, "col"), grad_down), axis=0)
    gain_total = gain_parts[0] + swap(gain_parts[1])
    own = jnp.where(first, result0, result1)
    other = swap(jnp.where(first, result1, result0))
    result = jnp.where(first, jnp.concatenate([own, other]), jnp.concatenate([other, own]))
    return (result[None], gain_total[None], grad_gate[None], grad_up[None], grad_down[None])


def solution(mesh):
    placed = (
        P("section", "col", "row"),
        P("section", "row"),
        P("section", "row", "col"),
        P("section", "row", "col"),
        P("section", "row", "col"),
        P("section", "row", "col"),
        P("section", "col", "row"),
        P("col", "row"),
    )
    return jax.shard_map(
        body,
        mesh=mesh,
        in_specs=placed,
        out_specs=(
            P("section", "col", "row"),
            P("section", "row"),
            P("section", "row", "col"),
            P("section", "row", "col"),
            P("section", "col", "row"),
        ),
        check_vma=False,
    )
```

```python
import jax
import jax.numpy as jnp
from jax import lax
from jax.sharding import PartitionSpec as P

D = 8192
EPSILON = 1e-05

bf16 = jnp.bfloat16
f32 = jnp.float32


def dot(left, right, dims):
    return lax.dot_general(left, right, (dims, ((), ())), preferred_element_type=f32)


def swap(block):
    return lax.ppermute(block, "section", [(0, 1), (1, 0)])


def after(block, event):
    return lax.optimization_barrier((block, event))[0]


def exchange(blocks, axis):
    return lax.all_to_all(blocks, axis, 0, 0)


def spread(block, axis):
    copies = jnp.broadcast_to(block[None], (lax.axis_size(axis),) + block.shape)
    return exchange(copies, axis)


def unit_grads(hidden_grad, saved):
    grad_f = hidden_grad.astype(f32)
    gate_f, up_f = saved[0].astype(f32), saved[1].astype(f32)
    sig = jax.nn.sigmoid(gate_f)
    gate_grad = (grad_f * up_f * sig * (1.0 + gate_f * (1.0 - sig))).astype(bf16)
    up_grad = (grad_f * gate_f * sig).astype(bf16)
    return gate_grad, up_grad


def into_features(gate_grad, up_grad, gate_w, up_w):
    partial = dot(gate_grad, gate_w, ((1,), (1,))) + dot(up_grad, up_w, ((1,), (1,)))
    return partial.astype(bf16)


def body(hidden_in, norm_gain, gate_saved, up_saved, w_gate, w_up, w_down, out_grad):
    rows, cols = lax.axis_size("row"), lax.axis_size("col")
    first = lax.axis_index("section") == 0
    features = hidden_in.shape[2]
    units = gate_saved.shape[2]
    half = hidden_in.shape[1] // 2

    def mine_theirs(block):
        low, high = block[:half], block[half:]
        return jnp.where(first, low, high), jnp.where(first, high, low)

    def by_layer(own, other):
        return jnp.where(first, other, own), jnp.where(first, own, other)

    gate_blocks = gate_saved[0].reshape(2, 2, half, units)
    up_blocks = up_saved[0].reshape(2, 2, half, units)
    saved = jnp.stack([gate_blocks, up_blocks])
    saved_low, saved_high = saved[:, :, 0], saved[:, :, 1]
    saved_mine = jnp.where(first, saved_low, saved_high)
    saved_other = swap(jnp.where(first, saved_high, saved_low))

    def gather_saved(block):
        block = block.reshape(2, 1, 2 * half, units)
        return lax.all_gather(block, "row", axis=2, tiled=True)

    saved1, saved0 = by_layer(saved_mine, saved_other)
    down_own = w_down[0]
    down_swapped = swap(after(down_own, saved_other))
    down1 = after(jnp.where(first, down_swapped, down_own), saved1)
    hid_mine, hid_theirs = mine_theirs(hidden_in[0])
    hid_other = swap(hid_theirs)
    gain1, gain0 = by_layer(norm_gain[0], swap(norm_gain[0]))
    hid1, hid0 = by_layer(hid_mine, hid_other)

    def scatter_units(cot, down_w):
        cot_all = spread(cot, "col").reshape(cols * half, features)
        return cot_all, dot(cot_all, down_w, ((1,), (1,))).astype(bf16)

    def gather_units(partial):
        pieces = exchange(partial.reshape(rows, 2 * half, units), "row")
        return jnp.sum(pieces.astype(f32), axis=0).astype(bf16)

    def all_units(grad_local):
        return spread(grad_local, "row").reshape(cols * half, units)

    def normed_grads(partial):
        pieces = exchange(partial.reshape(cols, half, features), "col")
        return jnp.sum(pieces.astype(f32), axis=0)

    def inner(normed_grad, hidden, gain):
        return jnp.sum(gain * normed_grad * hidden.astype(f32), axis=1)

    def over_rows(sums):
        return jnp.sum(spread(sums.reshape(1, -1), "row"), axis=0)[0]

    def finish(cot, normed_grad, hidden, inv_rms, gain, cross):
        return (
            cot.astype(f32)
            + inv_rms[:, None] * gain * normed_grad
            - hidden.astype(f32) * (inv_rms**3 * cross / D)[:, None]
        ).astype(bf16)

    def gain_part(normed_grad, hidden, inv_rms):
        return jnp.sum(normed_grad * hidden.astype(f32) * inv_rms[:, None], axis=0)

    def activation(saved):
        gate_f = saved[0].astype(f32)
        return (gate_f * jax.nn.sigmoid(gate_f) * saved[1].astype(f32)).astype(bf16)

    def both_halves(layer1, layer0, event):
        layer1, layer0, _ = lax.optimization_barrier((layer1, layer0, event))
        own = jnp.where(first, layer0, layer1)
        other = swap(jnp.where(first, layer1, layer0))
        return own, other

    def handed(block, source, target):
        return lax.ppermute(block, "section", [(source, target)])

    saved1 = gather_saved(saved1)
    cot1 = mine_theirs(out_grad)[0]
    cot_all1, partial = scatter_units(cot1, down1)
    gate_own, up_own = w_gate[0], w_up[0]
    gate_swapped = swap(after(gate_own, cot_all1))
    up_swapped = swap(after(up_own, cot_all1))
    grad_local = gather_units(partial)
    gates1 = lax.optimization_barrier(jnp.where(first, gate_swapped, gate_own))
    ups1 = lax.optimization_barrier(jnp.where(first, up_swapped, up_own))
    both = jnp.concatenate([hid_mine, hid_theirs, hid_other], axis=0).astype(f32)
    squares = after(jnp.sum(both * both, axis=1), grad_local)

    grad_local = after(grad_local, saved1)
    hidden_grad1 = all_units(grad_local)
    gate_grad1, up_grad1 = unit_grads(hidden_grad1, saved1[:, 0])
    partial = into_features(gate_grad1, up_grad1, gates1, ups1)
    saved0 = gather_saved(after(saved0, gate_grad1))
    normed_grad1 = normed_grads(partial)
    sums = over_rows(jnp.concatenate([squares, inner(normed_grad1, hid1, gain1)]))
    inv = lax.rsqrt(sums[: 3 * half] / D + EPSILON)
    inv1, inv0 = by_layer(inv[:half], inv[2 * half :])
    result1 = finish(cot1, normed_grad1, hid1, inv1, gain1, sums[3 * half :])

    down0 = jnp.where(first, *lax.optimization_barrier((down_own, down_swapped, result1))[:2])
    cot_all0, partial = scatter_units(result1, lax.optimization_barrier(down0))
    partial = after(partial, saved0)
    normed = jnp.concatenate([hid_mine, hid_theirs], axis=0).astype(f32)
    normed = normed * inv[: 2 * half, None] * norm_gain[0]
    normed = after(normed.astype(bf16).reshape(2, half, features), cot_all0)
    normed = lax.all_gather(normed, "col", axis=1, tiled=True)
    grad_local = gather_units(partial)
    hidden_grad0 = all_units(grad_local)
    grad_late = handed(hidden_grad0, 1, 0)
    saved_own, saved_theirs = both_halves(saved1[:, 0], saved0[:, 0], cot_all0)
    cot_own, cot_theirs = both_halves(cot_all1, cot_all0, cot_all0)
    grad_early = handed(after(hidden_grad1, cot_all0), 0, 1)
    weights = lax.optimization_barrier((gate_own, gate_swapped, up_own, up_swapped, grad_local))
    gates0 = lax.optimization_barrier(jnp.where(first, weights[0], weights[1]))
    ups0 = lax.optimization_barrier(jnp.where(first, weights[2], weights[3]))
    ready = (saved_theirs, cot_theirs, grad_early, gates0, ups0)
    gate_grad0, up_grad0 = unit_grads(after(hidden_grad0, ready), saved0[:, 0])
    partial = after(into_features(gate_grad0, up_grad0, gates0, ups0), normed)
    normed_grad0 = normed_grads(partial)
    grad_theirs = after(jnp.where(first, grad_late, grad_early), partial)
    gate_theirs, up_theirs = unit_grads(grad_theirs, saved_theirs)
    gate0, gate1, up0, up1 = after((gate_grad0, gate_grad1, up_grad0, up_grad1), partial)
    gate_own, up_own = jnp.where(first, gate0, gate1), jnp.where(first, up0, up1)
    gate_grads = jnp.concatenate([gate_own, gate_theirs], axis=0)
    up_grads = jnp.concatenate([up_own, up_theirs], axis=0)
    saved_own, saved_late, cot_own, cot_theirs = after((saved_own, saved_theirs, cot_own, cot_theirs), normed_grad0)
    acts = jnp.concatenate([activation(saved_own), activation(saved_late)], axis=0)
    grad_down = dot(acts, jnp.concatenate([cot_own, cot_theirs], axis=0), ((0,), (0,))).astype(bf16)
    cross = inner(normed_grad0, hid0, gain0)
    others = [lax.ppermute(cross, "row", [(i, i ^ bits) for i in range(rows)]) for bits in (1, 2, 3)]
    cross = cross + others[0] + others[1] + others[2]
    cross = cross + lax.ppermute(cross, "row", [(i, i ^ 4) for i in range(rows)])
    result0 = finish(result1, normed_grad0, hid0, inv0, gain0, cross)

    tokens = 2 * half * cols
    normed = normed.reshape(tokens, features)
    grad_gate = dot(normed, gate_grads, ((0,), (0,))).astype(bf16)
    grad_up = dot(normed, up_grads, ((0,), (0,))).astype(bf16)

    gain1_part = gain_part(normed_grad1, hid1, inv1)
    gain0_part = gain_part(normed_grad0, hid0, inv0)
    gain_parts = jnp.stack([jnp.where(first, gain0_part, gain1_part), jnp.where(first, gain1_part, gain0_part)])
    gain_parts = jnp.sum(after(spread(gain_parts, "col"), grad_down), axis=0)
    gain_total = gain_parts[0] + swap(gain_parts[1])
    own = jnp.where(first, result0, result1)
    other = swap(jnp.where(first, result1, result0))
    result = jnp.where(first, jnp.concatenate([own, other]), jnp.concatenate([other, own]))
    return (result[None], gain_total[None], grad_gate[None], grad_up[None], grad_down[None])


def solution(mesh):
    placed = (
        P("section", "col", "row"),
        P("section", "row"),
        P("section", "row", "col"),
        P("section", "row", "col"),
        P("section", "row", "col"),
        P("section", "row", "col"),
        P("section", "col", "row"),
        P("col", "row"),
    )
    return jax.shard_map(
        body,
        mesh=mesh,
        in_specs=placed,
        out_specs=(
            P("section", "col", "row"),
            P("section", "row"),
            P("section", "row", "col"),
            P("section", "row", "col"),
            P("section", "col", "row"),
        ),
        check_vma=False,
    )
```

```python
import jax
import jax.numpy as jnp
from jax import lax
from jax.sharding import PartitionSpec as P

D = 8192
EPSILON = 1e-05

bf16 = jnp.bfloat16
f32 = jnp.float32


def dot(left, right, dims):
    return lax.dot_general(left, right, (dims, ((), ())), preferred_element_type=f32)


def swap(block):
    return lax.ppermute(block, "section", [(0, 1), (1, 0)])


def after(block, event):
    return lax.optimization_barrier((block, event))[0]


def exchange(blocks, axis):
    return lax.all_to_all(blocks, axis, 0, 0)


def spread(block, axis):
    copies = jnp.broadcast_to(block[None], (lax.axis_size(axis),) + block.shape)
    return exchange(copies, axis)


def unit_grads(hidden_grad, saved):
    grad_f = hidden_grad.astype(f32)
    gate_f, up_f = saved[0].astype(f32), saved[1].astype(f32)
    sig = jax.nn.sigmoid(gate_f)
    gate_grad = (grad_f * up_f * sig * (1.0 + gate_f * (1.0 - sig))).astype(bf16)
    up_grad = (grad_f * gate_f * sig).astype(bf16)
    return gate_grad, up_grad


def into_features(gate_grad, up_grad, gate_w, up_w):
    partial = dot(gate_grad, gate_w, ((1,), (1,))) + dot(up_grad, up_w, ((1,), (1,)))
    return partial.astype(bf16)


def body(hidden_in, norm_gain, gate_saved, up_saved, w_gate, w_up, w_down, out_grad):
    rows, cols = lax.axis_size("row"), lax.axis_size("col")
    first = lax.axis_index("section") == 0
    features = hidden_in.shape[2]
    units = gate_saved.shape[2]
    half = hidden_in.shape[1] // 2

    def mine_theirs(block):
        low, high = block[:half], block[half:]
        return jnp.where(first, low, high), jnp.where(first, high, low)

    def by_layer(own, other):
        return jnp.where(first, other, own), jnp.where(first, own, other)

    gate_blocks = gate_saved[0].reshape(2, 2, half, units)
    up_blocks = up_saved[0].reshape(2, 2, half, units)
    saved = jnp.stack([gate_blocks, up_blocks])
    saved_low, saved_high = saved[:, :, 0], saved[:, :, 1]
    saved_mine = jnp.where(first, saved_low, saved_high)
    saved_other = swap(jnp.where(first, saved_high, saved_low))

    def gather_saved(block):
        block = block.reshape(2, 1, 2 * half, units)
        return lax.all_gather(block, "row", axis=2, tiled=True)

    saved1, saved0 = by_layer(saved_mine, saved_other)
    down_own = w_down[0]
    down_swapped = swap(after(down_own, saved_other))
    down1 = after(jnp.where(first, down_swapped, down_own), saved1)
    hid_mine, hid_theirs = mine_theirs(hidden_in[0])
    hid_other = swap(hid_theirs)
    gain1, gain0 = by_layer(norm_gain[0], swap(norm_gain[0]))
    hid1, hid0 = by_layer(hid_mine, hid_other)

    def scatter_units(cot, down_w):
        cot_all = spread(cot, "col").reshape(cols * half, features)
        return cot_all, dot(cot_all, down_w, ((1,), (1,))).astype(bf16)

    def gather_units(partial):
        pieces = exchange(partial.reshape(rows, 2 * half, units), "row")
        return jnp.sum(pieces.astype(f32), axis=0).astype(bf16)

    def all_units(grad_local):
        return spread(grad_local, "row").reshape(cols * half, units)

    def normed_grads(partial, beside=()):
        pieces = after(exchange(partial.reshape(cols, half, features), "col"), beside)
        return jnp.sum(pieces.astype(f32), axis=0)

    def inner(normed_grad, hidden, gain):
        return jnp.sum(gain * normed_grad * hidden.astype(f32), axis=1)

    def over_rows(sums):
        return jnp.sum(spread(sums.reshape(1, -1), "row"), axis=0)[0]

    def finish(cot, normed_grad, hidden, inv_rms, gain, cross):
        return (
            cot.astype(f32)
            + inv_rms[:, None] * gain * normed_grad
            - hidden.astype(f32) * (inv_rms**3 * cross / D)[:, None]
        ).astype(bf16)

    def gain_part(normed_grad, hidden, inv_rms):
        return jnp.sum(normed_grad * hidden.astype(f32) * inv_rms[:, None], axis=0)

    def activation(saved):
        gate_f = saved[0].astype(f32)
        return (gate_f * jax.nn.sigmoid(gate_f) * saved[1].astype(f32)).astype(bf16)

    def both_halves(layer1, layer0, event):
        layer1, layer0, _ = lax.optimization_barrier((layer1, layer0, event))
        own = jnp.where(first, layer0, layer1)
        other = swap(jnp.where(first, layer1, layer0))
        return own, other

    def handed(block, source, target):
        return lax.ppermute(block, "section", [(source, target)])

    saved1 = gather_saved(saved1)
    cot1 = mine_theirs(out_grad)[0]
    cot_all1, partial = scatter_units(cot1, down1)
    gate_own, up_own = w_gate[0], w_up[0]
    gate_swapped = swap(after(gate_own, cot_all1))
    up_swapped = swap(after(up_own, cot_all1))
    grad_local = gather_units(partial)
    gates1 = lax.optimization_barrier(jnp.where(first, gate_swapped, gate_own))
    ups1 = lax.optimization_barrier(jnp.where(first, up_swapped, up_own))
    both = jnp.concatenate([hid_mine, hid_theirs, hid_other], axis=0).astype(f32)
    squares = after(jnp.sum(both * both, axis=1), grad_local)

    grad_local = after(grad_local, saved1)
    hidden_grad1 = all_units(grad_local)
    gate_grad1, up_grad1 = unit_grads(hidden_grad1, saved1[:, 0])
    partial = into_features(gate_grad1, up_grad1, gates1, ups1)
    saved0 = gather_saved(after(saved0, gate_grad1))
    weights = after((gate_own, gate_swapped, up_own, up_swapped), partial)
    gates0 = lax.optimization_barrier(jnp.where(first, weights[0], weights[1]))
    ups0 = lax.optimization_barrier(jnp.where(first, weights[2], weights[3]))
    normed_grad1 = normed_grads(partial, (gates0, ups0))
    sums = over_rows(jnp.concatenate([squares, inner(normed_grad1, hid1, gain1)]))
    inv = lax.rsqrt(sums[: 3 * half] / D + EPSILON)
    inv1, inv0 = by_layer(inv[:half], inv[2 * half :])
    result1 = finish(cot1, normed_grad1, hid1, inv1, gain1, sums[3 * half :])

    down0 = jnp.where(first, *lax.optimization_barrier((down_own, down_swapped, result1))[:2])
    cot_all0, partial = scatter_units(result1, lax.optimization_barrier(down0))
    partial = after(partial, saved0)
    normed = jnp.concatenate([hid_mine, hid_theirs], axis=0).astype(f32)
    normed = normed * inv[: 2 * half, None] * norm_gain[0]
    normed = after(normed.astype(bf16).reshape(2, half, features), cot_all0)
    normed = lax.all_gather(normed, "col", axis=1, tiled=True)
    grad_local = gather_units(partial)
    hidden_grad0 = all_units(grad_local)
    grad_late = handed(hidden_grad0, 1, 0)
    saved_own, saved_theirs = both_halves(saved1[:, 0], saved0[:, 0], cot_all0)
    cot_own, cot_theirs = both_halves(cot_all1, cot_all0, cot_all0)
    grad_early = handed(after(hidden_grad1, cot_all0), 0, 1)
    acts = jnp.concatenate([activation(saved_own), activation(saved_theirs)], axis=0)
    grad_down = dot(acts, jnp.concatenate([cot_own, cot_theirs], axis=0), ((0,), (0,))).astype(bf16)
    ready = (saved_theirs, grad_down, grad_early)
    gate_grad0, up_grad0 = unit_grads(after(hidden_grad0, ready), saved0[:, 0])
    partial = after(into_features(gate_grad0, up_grad0, gates0, ups0), normed)
    normed_grad0 = normed_grads(partial)
    grad_theirs = after(jnp.where(first, grad_late, grad_early), partial)
    gate_theirs, up_theirs = unit_grads(grad_theirs, saved_theirs)
    gate0, gate1, up0, up1 = after((gate_grad0, gate_grad1, up_grad0, up_grad1), partial)
    gate_own, up_own = jnp.where(first, gate0, gate1), jnp.where(first, up0, up1)
    gate_grads = jnp.concatenate([gate_own, gate_theirs], axis=0)
    up_grads = jnp.concatenate([up_own, up_theirs], axis=0)
    cross = inner(normed_grad0, hid0, gain0)
    others = [lax.ppermute(cross, "row", [(i, i ^ bits) for i in range(rows)]) for bits in (1, 2, 3)]
    cross = cross + others[0] + others[1] + others[2]
    cross = cross + lax.ppermute(cross, "row", [(i, i ^ 4) for i in range(rows)])
    result0 = finish(result1, normed_grad0, hid0, inv0, gain0, cross)

    tokens = 2 * half * cols
    normed = normed.reshape(tokens, features)
    grad_gate = dot(normed, gate_grads, ((0,), (0,))).astype(bf16)
    grad_up = dot(normed, up_grads, ((0,), (0,))).astype(bf16)

    gain1_part = gain_part(normed_grad1, hid1, inv1)
    gain0_part = gain_part(normed_grad0, hid0, inv0)
    gain_parts = jnp.stack([jnp.where(first, gain0_part, gain1_part), jnp.where(first, gain1_part, gain0_part)])
    gain_parts = jnp.sum(spread(gain_parts, "col"), axis=0)
    gain_total = gain_parts[0] + swap(gain_parts[1])
    own = jnp.where(first, result0, result1)
    other = swap(jnp.where(first, result1, result0))
    result = jnp.where(first, jnp.concatenate([own, other]), jnp.concatenate([other, own]))
    return (result[None], gain_total[None], grad_gate[None], grad_up[None], grad_down[None])


def solution(mesh):
    placed = (
        P("section", "col", "row"),
        P("section", "row"),
        P("section", "row", "col"),
        P("section", "row", "col"),
        P("section", "row", "col"),
        P("section", "row", "col"),
        P("section", "col", "row"),
        P("col", "row"),
    )
    return jax.shard_map(
        body,
        mesh=mesh,
        in_specs=placed,
        out_specs=(
            P("section", "col", "row"),
            P("section", "row"),
            P("section", "row", "col"),
            P("section", "row", "col"),
            P("section", "col", "row"),
        ),
        check_vma=False,
    )
```
